32 devices in a mesh: seq: 16 (over z, y, x), grp: 2 (over core).
Axes of the slice: x: 2, y: 2, z: 4, core: 2. Of those that a mesh axis runs over, the one named last changes fastest.
Arguments:
- token_ids: int32 [6144], P('seq'), may hold values from 0 to 11
- streams: bfloat16 [3, 6144, 1024], P(None, 'seq', 'grp'), may hold values from -20 to 20
- log_decay: float32 [8, 6144], P('grp', 'seq'), may hold values from -0.7 to 0, as said below
- beta_table: float32 [12, 8], replicated, may hold values from -4 to 4
- conv_weight: float32 [6, 3, 3, 1024], P(None, None, None, 'grp'), may hold values from -2.5 to 2.5
- cotangent: bfloat16 [6144, 1024], P('seq', 'grp'), may hold values from -6 to 6
Outputs:
- mixed_out: bfloat16 [6144, 1024], P('seq', 'grp')
- grad_streams: bfloat16 [3, 6144, 1024], P(None, 'seq', 'grp')
- grad_decay: float32 [8, 6144], P('grp', 'seq')
The draws below stay inside these ranges and needn't reach their ends.
Inputs may be any that keep to these rules, and one draw needn't show every extreme that they name: `log_decay`: every entry is negative.
All inputs are finite; a program needn't handle non-finite values.
Results may differ from the reference program's by a relative error of at most 0.00275.
Values may be sent and summed in bfloat16 or wider, within the bound.
A program may use at most 128 MiB of HBM per device.

```python
import math
import jax
import jax.numpy as jnp
from jax import lax

H = 8
DK = 128
VOCAB = 12
LCONV = 6
ROWS = 384
HALO = 126
CH = 1024
TOKENS = 6144


def draw_streams(key, part):
    key = jax.random.fold_in(key, 11)
    key_entries, key_norm_factors = jax.random.split(key, 2)
    channel_count = H * DK
    lowest = jnp.array([math.log(0.3), math.log(0.003), math.log(0.3)], jnp.float32)[:, None] * jnp.ones((1, channel_count), jnp.float32)
    highest = jnp.array([math.log(3.0), 0.0, math.log(3.0)], jnp.float32)[:, None] * jnp.ones((1, channel_count), jnp.float32)
    scales = jnp.exp(lowest + (highest - lowest) * jax.random.uniform(key_norm_factors, (3, channel_count), jnp.float32))
    entries = jnp.clip(jax.random.normal(key_entries, (3, TOKENS, channel_count), jnp.float32), -6.0, 6.0)
    return (entries * scales[:, None, :]).astype(jnp.bfloat16)


def draw_log_decay(key, part):
    key = jax.random.fold_in(key, 23)
    key_kind, key_fast, key_slow, key_rough, key_spots, key_drops = jax.random.split(key, 6)
    share_fast = 0.5
    is_fast = jax.random.uniform(key_kind, (H,), jnp.float32) < share_fast
    fast_rate = 1.0 / jax.random.uniform(key_fast, (H,), jnp.float32, 30.0, 50.0)
    slow_rate = jnp.exp(jax.random.uniform(key_slow, (H,), jnp.float32, math.log(0.05), 0.0)) / TOKENS
    rate = jnp.where(is_fast, fast_rate, slow_rate)
    rough = jnp.exp(jax.random.uniform(key_rough, (H, TOKENS), jnp.float32, math.log(0.5), math.log(2.0)))
    decay_factors = -rate[:, None] * rough
    spots = jax.random.randint(key_spots, (H, 2), 0, TOKENS)
    dropped_terms = jnp.log(jax.random.uniform(key_drops, (H, 2), jnp.float32, 0.5, 0.8))
    places = jnp.arange(TOKENS)
    masked_entries = places[None, :, None] == spots[:, None, :]
    expanded_tokens = jnp.min(jnp.where(masked_entries, dropped_terms[:, None, :], 0.0), axis=2)
    decay_factors = jnp.where(jnp.any(masked_entries, axis=2), expanded_tokens, decay_factors)
    return decay_factors.astype(jnp.float32)


def plant(values, stream_key, smallest, high):
    dims = values.shape
    index_at = [jax.random.randint(jax.random.fold_in(stream_key, axis), (), 0, dims[axis]) for axis in range(len(dims))]
    values = values.at[tuple(index_at)].set(smallest)
    longest = dims.index(max(dims))
    index_at[longest] = (index_at[longest] + 1) % dims[longest]
    return values.at[tuple(index_at)].set(high)


def level_of(key, shape, shards, least, top_value):
    loudness, own = 1.0, jax.random.fold_in(key, 6)
    for axis_at, parts in shards:
        steps = jnp.exp(jax.random.uniform(jax.random.fold_in(own, axis_at), (parts,), jnp.float32, least / len(shards), top_value / len(shards)))
        loudness = loudness * jnp.repeat(steps, shape[axis_at] // parts).reshape([-1 if axis == axis_at else 1 for axis in range(len(shape))])
    return loudness


def bell_draw(rng, dims, width, reach, shards=(), kind=jnp.bfloat16):
    result = jax.random.normal(rng, dims, jnp.float32) * width
    if len(shards) > 0:
        result = level_of(rng, dims, shards, -0.22, 0.18) * result
    return jnp.clip(result, min=-reach, max=reach).astype(kind)


def setup_inputs(seed: int = 0) -> dict:
    key_of = jax.random.split(jax.random.key(seed), 7)
    token_ids = plant(jax.random.randint(key_of[0], (TOKENS,), 0, VOCAB), jax.random.fold_in(key_of[0], 1), 0, VOCAB - 1).astype(jnp.int32)
    streams = draw_streams(jax.random.fold_in(key_of[6], 71), 0)
    log_decay = draw_log_decay(jax.random.fold_in(key_of[6], 71), 0)
    beta_table = bell_draw(key_of[3], (VOCAB, H), 1.5, 4.0, (), jnp.float32)
    conv_weight = bell_draw(key_of[4], (LCONV, 3, 3, CH), 0.6, 2.5, ((3, 2),), jnp.float32)
    cotangent = bell_draw(key_of[5], (TOKENS, CH), 1.0, 6.0, ((0, 16), (1, 2)))
    return {"token_ids": token_ids, "streams": streams, "log_decay": log_decay, "beta_table": beta_table, "conv_weight": conv_weight, "cotangent": cotangent}


PRECISE = lax.Precision.HIGHEST
EPSILON = 1e-06

def conv_stack(extended, conv_weight):
    current = extended
    extent = current.shape[0]
    for layer_index in range(conv_weight.shape[0]):
        spacing = 2 ** layer_index
        padded = jnp.pad(current, ((2 * spacing, 0), (0, 0)))
        summed = conv_weight[layer_index, 0] * current + conv_weight[layer_index, 1] * padded[spacing:spacing + extent] + conv_weight[layer_index, 2] * padded[:extent]
        current = current + jax.nn.silu(summed)
    return current

def unit_heads(columns, head_count):
    extent = columns.shape[0]
    split_up = columns.reshape(extent, head_count, -1).transpose(1, 0, 2)
    return split_up * lax.rsqrt(lax.optimization_barrier(jnp.sum(split_up * split_up, axis=2, keepdims=True)) + EPSILON)

def prepare(extended, log_decay, beta_gate, conv_weight):
    head_count = log_decay.shape[0]
    length = log_decay.shape[1]
    margin = extended.shape[0] - length
    convolution_output = jax.checkpoint(conv_stack)(extended, conv_weight)[margin:]
    stream_width = convolution_output.shape[1] // 3
    queries = unit_heads(convolution_output[:, :stream_width], head_count)
    keyvec = unit_heads(convolution_output[:, stream_width:2 * stream_width], head_count)
    values = convolution_output[:, 2 * stream_width:].reshape(length, head_count, -1).transpose(1, 0, 2)
    positions = jnp.arange(length)
    upper_ones = (positions[:, None] <= positions[None, :]).astype(jnp.float32)
    cumulative = jnp.dot(log_decay, upper_ones, precision=PRECISE)
    strict_lower_mask = positions[:, None] > positions[None, :]
    log_gaps = jnp.where(strict_lower_mask[None], cumulative[:, :, None] - cumulative[:, None, :], 0.0)
    affinity = jnp.einsum('htk,hsk->hts', keyvec, keyvec, precision=PRECISE)
    lower_part = jnp.where(strict_lower_mask[None], jnp.exp(log_gaps) * affinity, 0.0)
    system = jnp.eye(length, dtype=jnp.float32)[None] + beta_gate[:, :, None] * lower_part
    pseudo = jax.scipy.linalg.solve_triangular(system, beta_gate[:, :, None] * values, lower=True, unit_diagonal=True)
    keyed_rows = jax.scipy.linalg.solve_triangular(system, (beta_gate * jnp.exp(cumulative))[:, :, None] * keyvec, lower=True, unit_diagonal=True)
    group_total = cumulative[:, -1]
    remain = jnp.exp(group_total[:, None] - cumulative)
    dimension = keyvec.shape[2]
    transition = jnp.exp(group_total)[:, None, None] * jnp.eye(dimension, dtype=jnp.float32)[None] - jnp.einsum('htk,ht,htj->hkj', keyed_rows, remain, keyvec, precision=PRECISE)
    group_state = jnp.einsum('htv,ht,htk->hvk', pseudo, remain, keyvec, precision=PRECISE)
    return (queries, keyvec, cumulative, pseudo, keyed_rows, transition, group_state)

def finish(pieces, entering):
    queries, keyvec, cumulative, pseudo, keyed_rows, transition, group_state = pieces
    length = cumulative.shape[1]
    positions = jnp.arange(length)
    within = positions[:, None] >= positions[None, :]
    log_gaps = jnp.where(within[None], cumulative[:, :, None] - cumulative[:, None, :], 0.0)
    intersection = jnp.einsum('htk,hsk->hts', queries, keyvec, precision=PRECISE)
    weights = jnp.where(within[None], jnp.exp(log_gaps) * intersection, 0.0)
    written = pseudo - jnp.einsum('htk,hvk->htv', keyed_rows, entering, precision=PRECISE)
    scaling = queries.shape[2] ** (-0.5)
    carried_in = jnp.exp(cumulative)[:, :, None] * jnp.einsum('htk,hvk->htv', queries, entering, precision=PRECISE)
    outputs = scaling * (carried_in + jnp.einsum('hts,hsv->htv', weights, written, precision=PRECISE))
    leaving = jnp.einsum('hvk,hkj->hvj', entering, transition, precision=PRECISE) + group_state
    return (outputs, leaving)

def forward(streams_wide, log_decay, beta_gate, conv_weight):
    blocks = TOKENS // ROWS
    main_rows = streams_wide.reshape(blocks, ROWS, -1)
    tails = jnp.concatenate([jnp.zeros((1, HALO, main_rows.shape[2]), jnp.float32), main_rows[:-1, ROWS - HALO:]], 0)
    extended = jnp.concatenate([tails, main_rows], 1)
    blocked_decay_factors = log_decay.reshape(H, blocks, ROWS).transpose(1, 0, 2)
    beta_blocks = beta_gate.reshape(H, blocks, ROWS).transpose(1, 0, 2)

    def pair_of(packed):
        pieces = prepare(packed[0], packed[1], packed[2], conv_weight)
        return (pieces[5], pieces[6])
    transitions, states = lax.map(jax.checkpoint(pair_of), (extended, blocked_decay_factors, beta_blocks))

    def advance(carried, packed):
        return (jnp.einsum('hvk,hkj->hvj', carried, packed[0], precision=PRECISE) + packed[1], carried)
    initial = jnp.zeros((H, DK, DK), jnp.float32)
    ignored, entering = lax.scan(advance, initial, (transitions, states))

    def output_of(packed):
        pieces = prepare(packed[0], packed[1], packed[2], conv_weight)
        return finish(pieces, packed[3])[0]
    outputs = lax.map(jax.checkpoint(output_of), (extended, blocked_decay_factors, beta_blocks, entering))
    return outputs.transpose(0, 2, 1, 3).reshape(TOKENS, H * DK)

def reference(token_ids, streams, log_decay, beta_table, conv_weight, cotangent):
    beta_gate = jax.nn.sigmoid(beta_table[token_ids]).T
    taps = conv_weight.reshape(LCONV, 3, 3 * CH)

    def whole_layer(streams_wide, decay_values):
        return forward(streams_wide, decay_values, beta_gate, taps)
    wide = streams.astype(jnp.float32).transpose(1, 0, 2).reshape(TOKENS, 3 * CH)
    mixed, backward = jax.vjp(whole_layer, wide, log_decay)
    grad_wide, grad_decay = backward(cotangent.astype(jnp.float32))
    grad_streams = grad_wide.reshape(TOKENS, 3, CH).transpose(1, 0, 2)
    return (mixed.astype(jnp.bfloat16), grad_streams.astype(jnp.bfloat16), grad_decay)
```

```python
import jax
import jax.numpy as jnp
from jax import lax
from jax.experimental import pallas as pl
from jax.experimental.pallas import tpu as pltpu
from jax.sharding import PartitionSpec as P
import functools

EXACT = lax.Precision.HIGHEST
PRECISE = lax.Precision.HIGH
TILE = 128
EPSILON = 1e-06


def shifted(value, axis, steps):
    count = lax.axis_size(axis)
    first, last = (max(0, -steps), min(count, count - steps))
    return lax.ppermute(value, axis, [(source, source + steps) for source in range(first, last)])


def halves(value):
    high = value.astype(jnp.bfloat16)
    low = (value - high.astype(jnp.float32)).astype(jnp.bfloat16)
    return high, low


def product(left, right, contract=(1, 0)):
    dims = (((contract[0],), (contract[1],)), ((), ()))

    def one(a, b):
        return lax.dot_general(a, b, dims, preferred_element_type=jnp.float32)

    return one(left[0], right[0]) + (one(left[0], right[1]) + one(left[1], right[0]))


def inverse_kernel(lower_ref, inverse_ref):
    length = lower_ref.shape[1]
    count = length // TILE
    rows = lax.broadcasted_iota(jnp.int32, (TILE, TILE), 0)
    columns = lax.broadcasted_iota(jnp.int32, (TILE, TILE), 1)
    identity = (rows == columns).astype(jnp.float32)
    exact = functools.partial(jnp.dot, precision=EXACT, preferred_element_type=jnp.float32)
    cells = [slice(b * TILE, (b + 1) * TILE) for b in range(count)]
    lowers = [lower_ref[0, cell, cell] for cell in cells]
    small = (rows // 8) == (columns // 8)
    firsts = [jnp.where(small, lower, 0.0) for lower in lowers]
    seconds = [exact(first, first) for first in firsts]
    fourths = [exact(second, second) for second in seconds]
    bases = [
        identity - first + second - exact(first, second) for first, second in zip(firsts, seconds)
    ]
    results = [base + exact(base, fourth) for base, fourth in zip(bases, fourths)]
    size = 8
    while size < TILE:
        joined = (rows // (2 * size) == columns // (2 * size)) & (rows // size != columns // size)
        offs = [halves(jnp.where(joined, lower, 0.0)) for lower in lowers]
        splits = [halves(result) for result in results]
        inner = [halves(product(off, split)) for off, split in zip(offs, splits)]
        results = [
            result - product(split, part) for result, split, part in zip(results, splits, inner)
        ]
        size *= 2
    splits = [halves(result) for result in results]
    found = {}
    for i in range(count):
        found[i, i] = splits[i]
        inverse_ref[0, cells[i], cells[i]] = results[i]
        for j in range(count):
            if j > i:
                inverse_ref[0, cells[i], cells[j]] = jnp.zeros((TILE, TILE), jnp.float32)
            if j < i:
                total = jnp.zeros((TILE, TILE), jnp.float32)
                for m in range(j, i):
                    total += product(halves(lower_ref[0, cells[i], cells[m]]), found[m, j])
                entry = -product(splits[i], halves(total))
                inverse_ref[0, cells[i], cells[j]] = entry
                found[i, j] = halves(entry)


def inverse_of(lower):
    heads, length, _ = lower.shape
    spec = pl.BlockSpec((1, length, length), lambda h: (h, 0, 0))
    return pl.pallas_call(
        inverse_kernel,
        grid=(heads,),
        in_specs=[spec],
        out_specs=spec,
        out_shape=jax.ShapeDtypeStruct(lower.shape, jnp.float32),
        compiler_params=pltpu.CompilerParams(vmem_limit_bytes=32 * 2**20),
        name="triangle_inverse",
    )(lower)


@jax.custom_vjp
def solved(lower, given):
    return solved_forward(lower, given)[0]


def solved_forward(lower, given):
    inverse = inverse_of(lower)
    found = jnp.einsum("hts,hsk->htk", inverse, given, precision=PRECISE)
    return found, (inverse, found)


def solved_backward(kept, upstream):
    inverse, found = kept
    given_grad = jnp.einsum("hts,htk->hsk", inverse, upstream, precision=PRECISE)
    lower_grad = -jnp.einsum("htk,hsk->hts", given_grad, found, precision=PRECISE)
    return lower_grad, given_grad


solved.defvjp(solved_forward, solved_backward)


def chain_kernel(
    blocks,
    maps,
    states,
    grads,
    entering,
    later,
    high,
    low,
    send_e,
    send_l,
    recv_e,
    recv_l,
    sent_e,
    came_e,
    sent_l,
    came_l,
):
    heads = maps.shape[0]
    me = lax.axis_index("seq")
    right = lax.rem(me + 1, blocks)
    left = lax.rem(me + blocks - 1, blocks)
    has_left = me > 0
    has_right = me < blocks - 1
    barrier = pltpu.get_barrier_semaphore()

    @pl.when(has_left)
    def _():
        pl.semaphore_signal(
            barrier, inc=1, device_id={"seq": left}, device_id_type=pl.DeviceIdType.MESH
        )

    @pl.when(has_right)
    def _():
        pl.semaphore_signal(
            barrier, inc=1, device_id={"seq": right}, device_id_type=pl.DeviceIdType.MESH
        )

    for head in range(heads):
        high[head], low[head] = halves(maps[head])

    @pl.when(has_left & has_right)
    def _():
        pl.semaphore_wait(barrier, 2)

    @pl.when(has_left != has_right)
    def _():
        pl.semaphore_wait(barrier, 1)

    def onward(head):
        return pltpu.make_async_remote_copy(
            src_ref=send_e.at[head],
            dst_ref=recv_e.at[head],
            send_sem=sent_e.at[head],
            recv_sem=came_e.at[head],
            device_id={"seq": right},
            device_id_type=pl.DeviceIdType.MESH,
        )

    def backward(head):
        return pltpu.make_async_remote_copy(
            src_ref=send_l.at[head],
            dst_ref=recv_l.at[head],
            send_sem=sent_l.at[head],
            recv_sem=came_l.at[head],
            device_id={"seq": left},
            device_id_type=pl.DeviceIdType.MESH,
        )

    def pass_on(copy, has_source, has_target, received, sending, kept, added, contract):
        for head in range(heads):

            @pl.when(has_source)
            def _():
                copy(head).wait_recv()
                value = received[head]
                kept[head] = value

                @pl.when(has_target)
                def _():
                    moved = product(halves(value), (high[head], low[head]), contract)
                    sending[head] = moved + added[head]
                    copy(head).start()

            @pl.when(jnp.logical_not(has_source))
            def _():
                kept[head] = jnp.zeros(kept.shape[1:], jnp.float32)

                @pl.when(has_target)
                def _():
                    sending[head] = added[head]
                    copy(head).start()

    def states_on():
        pass_on(onward, has_left, has_right, recv_e, send_e, entering, states, (1, 0))

    def grads_back():
        pass_on(backward, has_right, has_left, recv_l, send_l, later, grads, (1, 1))

    early = me < blocks // 2

    @pl.when(early)
    def _():
        states_on()
        grads_back()

    @pl.when(jnp.logical_not(early))
    def _():
        grads_back()
        states_on()

    for head in range(heads):

        @pl.when(has_right)
        def _():
            onward(head).wait_send()

        @pl.when(has_left)
        def _():
            backward(head).wait_send()


def chain(maps, states, grads):
    blocks = lax.axis_size("seq")
    heads = maps.shape[0]
    shape = jax.ShapeDtypeStruct(maps.shape, jnp.float32)
    spec = pl.BlockSpec(memory_space=pltpu.VMEM)
    return pl.pallas_call(
        functools.partial(chain_kernel, blocks),
        out_shape=(shape, shape),
        in_specs=[spec] * 3,
        out_specs=(spec, spec),
        scratch_shapes=[pltpu.VMEM(maps.shape, jnp.bfloat16)] * 2
        + [pltpu.VMEM(maps.shape, jnp.float32)] * 4
        + [pltpu.SemaphoreType.DMA((heads,))] * 4,
        compiler_params=pltpu.CompilerParams(
            collective_id=0, has_side_effects=True, vmem_limit_bytes=32 * 2**20
        ),
        name="state_chain",
    )(maps, states, grads)


def conv_stack(extended, conv_weight):
    current = extended
    extent = current.shape[0]
    for layer_index in range(conv_weight.shape[0]):
        spacing = 2**layer_index
        padded = jnp.pad(current, ((2 * spacing, 0), (0, 0)))
        summed = (
            conv_weight[layer_index, 0] * current
            + conv_weight[layer_index, 1] * padded[spacing : spacing + extent]
            + conv_weight[layer_index, 2] * padded[:extent]
        )
        current = current + jax.nn.silu(summed)
    return current


def unit_heads(columns, head_count):
    extent = columns.shape[0]
    split_up = columns.reshape(extent, head_count, -1).transpose(1, 0, 2)
    return split_up * lax.rsqrt(jnp.sum(split_up * split_up, axis=2, keepdims=True) + EPSILON)


def prepare(extended, log_decay, beta_gate, conv_weight):
    head_count = log_decay.shape[0]
    length = log_decay.shape[1]
    margin = extended.shape[0] - length
    convolution_output = jax.checkpoint(conv_stack)(extended, conv_weight)[margin:]
    stream_width = convolution_output.shape[1] // 3
    queries = unit_heads(convolution_output[:, :stream_width], head_count)
    keyvec = unit_heads(convolution_output[:, stream_width : 2 * stream_width], head_count)
    values = (
        convolution_output[:, 2 * stream_width :].reshape(length, head_count, -1).transpose(1, 0, 2)
    )
    positions = jnp.arange(length)
    upper_ones = (positions[:, None] <= positions[None, :]).astype(jnp.float32)
    cumulative = jnp.dot(log_decay, upper_ones, precision=EXACT)
    strict_lower_mask = positions[:, None] > positions[None, :]
    log_gaps = jnp.where(
        strict_lower_mask[None], cumulative[:, :, None] - cumulative[:, None, :], 0.0
    )
    affinity = jnp.einsum("htk,hsk->hts", keyvec, keyvec, precision=PRECISE)
    lower_part = jnp.where(strict_lower_mask[None], jnp.exp(log_gaps) * affinity, 0.0)
    dimension = keyvec.shape[2]
    given = jnp.concatenate(
        [beta_gate[:, :, None] * values, (beta_gate * jnp.exp(cumulative))[:, :, None] * keyvec], 2
    )
    found = solved(beta_gate[:, :, None] * lower_part, given)
    pseudo, keyed_rows = found[:, :, :dimension], found[:, :, dimension:]
    group_total = cumulative[:, -1]
    remain = jnp.exp(group_total[:, None] - cumulative)
    transition = jnp.exp(group_total)[:, None, None] * jnp.eye(dimension, dtype=jnp.float32)[
        None
    ] - jnp.einsum("htk,ht,htj->hkj", keyed_rows, remain, keyvec, precision=PRECISE)
    group_state = jnp.einsum("htv,ht,htk->hvk", pseudo, remain, keyvec, precision=PRECISE)
    return (queries, keyvec, cumulative, pseudo, keyed_rows, transition, group_state)


def finish(pieces, entering):
    queries, keyvec, cumulative, pseudo, keyed_rows, transition, group_state = pieces
    length = cumulative.shape[1]
    positions = jnp.arange(length)
    within = positions[:, None] >= positions[None, :]
    log_gaps = jnp.where(within[None], cumulative[:, :, None] - cumulative[:, None, :], 0.0)
    intersection = jnp.einsum("htk,hsk->hts", queries, keyvec, precision=PRECISE)
    weights = jnp.where(within[None], jnp.exp(log_gaps) * intersection, 0.0)
    written = pseudo - jnp.einsum("htk,hvk->htv", keyed_rows, entering, precision=PRECISE)
    scaling = queries.shape[2] ** (-0.5)
    carried_in = jnp.exp(cumulative)[:, :, None] * jnp.einsum(
        "htk,hvk->htv", queries, entering, precision=PRECISE
    )
    outputs = scaling * (
        carried_in + jnp.einsum("hts,hsv->htv", weights, written, precision=PRECISE)
    )
    leaving = jnp.einsum("hvk,hkj->hvj", entering, transition, precision=PRECISE) + group_state
    return (outputs, leaving)


def on_device(token_ids, streams, log_decay, beta_table, conv_weight, cotangent):
    length = streams.shape[1]
    width = streams.shape[2]
    head_count = log_decay.shape[0]
    margin = 2 * (2 ** conv_weight.shape[0] - 1)
    earlier_rows = shifted(streams[:, length - margin :], "seq", 1)
    joined = jnp.concatenate([earlier_rows, streams], 1)
    extended = joined.transpose(1, 0, 2).reshape(length + margin, 3 * width).astype(jnp.float32)
    taps = conv_weight.reshape(conv_weight.shape[0], 3, 3 * width)
    first_head = lax.axis_index("grp") * head_count
    own_table = lax.dynamic_slice_in_dim(beta_table, first_head, head_count, 1)
    letters = jnp.arange(beta_table.shape[0])
    one_hot = (letters[:, None] == token_ids[None, :]).astype(jnp.float32)
    beta_gate = jax.nn.sigmoid(jnp.dot(own_table.T, one_hot, precision=EXACT))

    def local_pieces(rows_given, decay_given):
        return prepare(rows_given, decay_given, beta_gate, taps)

    pieces, prepare_back = jax.vjp(local_pieces, extended, log_decay)
    upstream = cotangent.astype(jnp.float32).reshape(length, head_count, -1).transpose(1, 0, 2)
    nothing = jnp.zeros_like(pieces[6])
    state_grad = jax.vjp(lambda state: finish(pieces, state)[0], nothing)[1](upstream)[0]
    entering, later_grad = chain(pieces[5], pieces[6], state_grad)
    (outputs, leaving), finish_back = jax.vjp(finish, pieces, entering)
    summed, unused_grad = finish_back((upstream, later_grad))
    grad_extended, grad_decay = prepare_back(summed)
    grad_parts = grad_extended.reshape(length + margin, 3, width).transpose(1, 0, 2)
    returned = shifted(grad_parts[:, :margin].astype(jnp.bfloat16), "seq", -1).astype(jnp.float32)
    grad_own = grad_parts[:, margin:]
    grad_streams = jnp.concatenate(
        [grad_own[:, : length - margin], grad_own[:, length - margin :] + returned], 1
    )
    mixed_out = outputs.transpose(1, 0, 2).reshape(length, -1).astype(jnp.bfloat16)
    return (mixed_out, grad_streams.astype(jnp.bfloat16), grad_decay)


def solution(mesh):
    placed = (
        P("seq"),
        P(None, "seq", "grp"),
        P("grp", "seq"),
        P(),
        P(None, None, None, "grp"),
        P("seq", "grp"),
    )
    return jax.shard_map(
        on_device,
        mesh=mesh,
        in_specs=placed,
        out_specs=(P("seq", "grp"), P(None, "seq", "grp"), P("grp", "seq")),
        check_vma=False,
    )
```

```python
import jax
import jax.numpy as jnp
from jax import lax
from jax.experimental import pallas as pl
from jax.experimental.pallas import tpu as pltpu
from jax.sharding import PartitionSpec as P
import functools

EXACT = lax.Precision.HIGHEST
PRECISE = lax.Precision.HIGH
TILE = 128
EPSILON = 1e-06


def shifted(value, axis, steps):
    count = lax.axis_size(axis)
    first, last = (max(0, -steps), min(count, count - steps))
    return lax.ppermute(value, axis, [(source, source + steps) for source in range(first, last)])


def halves(value):
    high = value.astype(jnp.bfloat16)
    low = (value - high.astype(jnp.float32)).astype(jnp.bfloat16)
    return high, low


def product(left, right, contract=(1, 0)):
    dims = (((contract[0],), (contract[1],)), ((), ()))

    def one(a, b):
        return lax.dot_general(a, b, dims, preferred_element_type=jnp.float32)

    return one(left[0], right[0]) + (one(left[0], right[1]) + one(left[1], right[0]))


def inverse_kernel(lower_ref, inverse_ref):
    length = lower_ref.shape[1]
    count = length // TILE
    rows = lax.broadcasted_iota(jnp.int32, (TILE, TILE), 0)
    columns = lax.broadcasted_iota(jnp.int32, (TILE, TILE), 1)
    identity = (rows == columns).astype(jnp.float32)
    exact = functools.partial(jnp.dot, precision=EXACT, preferred_element_type=jnp.float32)
    cells = [slice(b * TILE, (b + 1) * TILE) for b in range(count)]
    heads = lower_ref.shape[0]
    lowers = [lower_ref[h, cell, cell] for h in range(heads) for cell in cells]
    small = (rows // 8) == (columns // 8)
    firsts = [jnp.where(small, lower, 0.0) for lower in lowers]
    seconds = [exact(first, first) for first in firsts]
    fourths = [exact(second, second) for second in seconds]
    bases = [
        identity - first + second - exact(first, second) for first, second in zip(firsts, seconds)
    ]
    results = [base + exact(base, fourth) for base, fourth in zip(bases, fourths)]
    size = 8
    while size < TILE:
        joined = (rows // (2 * size) == columns // (2 * size)) & (rows // size != columns // size)
        offs = [halves(jnp.where(joined, lower, 0.0)) for lower in lowers]
        splits = [halves(result) for result in results]
        inner = [halves(product(off, split)) for off, split in zip(offs, splits)]
        results = [
            result - product(split, part) for result, split, part in zip(results, splits, inner)
        ]
        size *= 2
    for h in range(heads):
        found = {}
        for i in range(count):
            own = results[h * count + i]
            own_split = halves(own)
            found[i, i] = own_split
            inverse_ref[h, cells[i], cells[i]] = own
            for j in range(i + 1, count):
                inverse_ref[h, cells[i], cells[j]] = jnp.zeros((TILE, TILE), jnp.float32)
            for j in range(i):
                total = jnp.zeros((TILE, TILE), jnp.float32)
                for m in range(j, i):
                    total += product(halves(lower_ref[h, cells[i], cells[m]]), found[m, j])
                entry = -product(own_split, halves(total))
                inverse_ref[h, cells[i], cells[j]] = entry
                found[i, j] = halves(entry)


def inverse_of(lower):
    spec = pl.BlockSpec(memory_space=pltpu.VMEM)
    return pl.pallas_call(
        inverse_kernel,
        in_specs=[spec],
        out_specs=spec,
        out_shape=jax.ShapeDtypeStruct(lower.shape, jnp.float32),
        compiler_params=pltpu.CompilerParams(vmem_limit_bytes=32 * 2**20),
        name="triangle_inverse",
    )(lower)


@jax.custom_vjp
def solved(lower, given):
    return solved_forward(lower, given)[0]


def solved_forward(lower, given):
    inverse = inverse_of(lower)
    found = jnp.einsum("hts,hsk->htk", inverse, given, precision=PRECISE)
    return found, (inverse, found)


def solved_backward(kept, upstream):
    inverse, found = kept
    given_grad = jnp.einsum("hts,htk->hsk", inverse, upstream, precision=PRECISE)
    lower_grad = -jnp.einsum("htk,hsk->hts", given_grad, found, precision=PRECISE)
    return lower_grad, given_grad


solved.defvjp(solved_forward, solved_backward)


def chain_kernel(
    blocks,
    maps,
    states,
    grads,
    entering,
    later,
    high,
    low,
    send_e,
    send_l,
    recv_e,
    recv_l,
    sent_e,
    came_e,
    sent_l,
    came_l,
):
    heads = maps.shape[0]
    me = lax.axis_index("seq")
    right = lax.rem(me + 1, blocks)
    left = lax.rem(me + blocks - 1, blocks)
    has_left = me > 0
    has_right = me < blocks - 1
    barrier = pltpu.get_barrier_semaphore()

    @pl.when(has_left)
    def _():
        pl.semaphore_signal(
            barrier, inc=1, device_id={"seq": left}, device_id_type=pl.DeviceIdType.MESH
        )

    @pl.when(has_right)
    def _():
        pl.semaphore_signal(
            barrier, inc=1, device_id={"seq": right}, device_id_type=pl.DeviceIdType.MESH
        )

    for head in range(heads):
        high[head], low[head] = halves(maps[head])

    @pl.when(has_left & has_right)
    def _():
        pl.semaphore_wait(barrier, 2)

    @pl.when(has_left != has_right)
    def _():
        pl.semaphore_wait(barrier, 1)

    def onward(head):
        return pltpu.make_async_remote_copy(
            src_ref=send_e.at[head],
            dst_ref=recv_e.at[head],
            send_sem=sent_e.at[head],
            recv_sem=came_e.at[head],
            device_id={"seq": right},
            device_id_type=pl.DeviceIdType.MESH,
        )

    def backward(head):
        return pltpu.make_async_remote_copy(
            src_ref=send_l.at[head],
            dst_ref=recv_l.at[head],
            send_sem=sent_l.at[head],
            recv_sem=came_l.at[head],
            device_id={"seq": left},
            device_id_type=pl.DeviceIdType.MESH,
        )

    def pass_on(copy, has_source, has_target, received, sending, kept, added, contract):
        for head in range(heads):

            @pl.when(has_source)
            def _():
                copy(head).wait_recv()
                value = received[head]
                kept[head] = value

                @pl.when(has_target)
                def _():
                    moved = product(halves(value), (high[head], low[head]), contract)
                    sending[head] = moved + added[head]
                    copy(head).start()

            @pl.when(jnp.logical_not(has_source))
            def _():
                kept[head] = jnp.zeros(kept.shape[1:], jnp.float32)

                @pl.when(has_target)
                def _():
                    sending[head] = added[head]
                    copy(head).start()

    def states_on():
        pass_on(onward, has_left, has_right, recv_e, send_e, entering, states, (1, 0))

    def grads_back():
        pass_on(backward, has_right, has_left, recv_l, send_l, later, grads, (1, 1))

    early = me < blocks // 2

    @pl.when(early)
    def _():
        states_on()
        grads_back()

    @pl.when(jnp.logical_not(early))
    def _():
        grads_back()
        states_on()

    for head in range(heads):

        @pl.when(has_right)
        def _():
            onward(head).wait_send()

        @pl.when(has_left)
        def _():
            backward(head).wait_send()


def chain(maps, states, grads):
    blocks = lax.axis_size("seq")
    heads = maps.shape[0]
    shape = jax.ShapeDtypeStruct(maps.shape, jnp.float32)
    spec = pl.BlockSpec(memory_space=pltpu.VMEM)
    return pl.pallas_call(
        functools.partial(chain_kernel, blocks),
        out_shape=(shape, shape),
        in_specs=[spec] * 3,
        out_specs=(spec, spec),
        scratch_shapes=[pltpu.VMEM(maps.shape, jnp.bfloat16)] * 2
        + [pltpu.VMEM(maps.shape, jnp.float32)] * 4
        + [pltpu.SemaphoreType.DMA((heads,))] * 4,
        compiler_params=pltpu.CompilerParams(
            collective_id=0, has_side_effects=True, vmem_limit_bytes=32 * 2**20
        ),
        name="state_chain",
    )(maps, states, grads)


def conv_kernel(margin, halo_ref, own_ref, taps_ref, out_ref, slope_ref):
    current = jnp.concatenate(
        [halo_ref[0].astype(jnp.float32), own_ref[0].astype(jnp.float32)], 0
    )
    for layer in range(slope_ref.shape[0]):
        spacing = 2**layer
        first, second, third = (taps_ref[0, 3 * layer + i : 3 * layer + i + 1, :] for i in range(3))
        summed = (
            first * current
            + second * pltpu.roll(current, spacing, 0)
            + third * pltpu.roll(current, 2 * spacing, 0)
        )
        gate = 0.5 * jnp.tanh(0.5 * summed) + 0.5
        slope_ref[layer, 0] = gate * (1.0 + summed * (1.0 - gate))
        current = current + summed * gate
    out_ref[0, 0] = current[margin:]


def conv_back_kernel(margin, grad_ref, slope_ref, taps_ref, halo_ref, own_ref):
    grad = grad_ref[0, 0]
    grad = jnp.concatenate([jnp.zeros((margin, grad.shape[1]), jnp.float32), grad], 0)
    extent = grad.shape[0]
    for layer in reversed(range(slope_ref.shape[0])):
        spacing = 2**layer
        first, second, third = (taps_ref[0, 3 * layer + i : 3 * layer + i + 1, :] for i in range(3))
        inner = grad * slope_ref[layer, 0]
        grad = (
            grad
            + first * inner
            + pltpu.roll(second * inner, extent - spacing, 0)
            + pltpu.roll(third * inner, extent - 2 * spacing, 0)
        )
    halo_ref[0] = grad[:margin].astype(jnp.bfloat16)
    own_ref[0] = grad[margin:]


def conv_specs(margin, length, dimension, layers):
    def columns(rows):
        return pl.BlockSpec((1, rows, dimension), lambda s, h: (s, 0, h))

    per_head = pl.BlockSpec((1, 1, length, dimension), lambda s, h: (s, h, 0, 0))
    slopes = pl.BlockSpec((layers, 1, margin + length, dimension), lambda s, h: (0, s, 0, h))
    return columns(margin), columns(length), columns(3 * layers), per_head, slopes


def conv_forward(halo, own, taps, heads):
    margin, length, width = halo.shape[1], own.shape[1], own.shape[2]
    layers, dimension = taps.shape[1] // 3, width // heads
    halo_spec, own_spec, taps_spec, per_head, slopes = conv_specs(margin, length, dimension, layers)
    return pl.pallas_call(
        functools.partial(conv_kernel, margin),
        grid=(3, heads),
        in_specs=[halo_spec, own_spec, taps_spec],
        out_specs=(per_head, slopes),
        out_shape=(
            jax.ShapeDtypeStruct((3, heads, length, dimension), jnp.float32),
            jax.ShapeDtypeStruct((layers, 3, margin + length, width), jnp.float32),
        ),
        compiler_params=pltpu.CompilerParams(vmem_limit_bytes=32 * 2**20),
        name="conv_forward",
    )(halo, own, taps)


def conv_backward(grad, slope, taps, margin):
    heads, length, dimension = grad.shape[1:]
    layers = slope.shape[0]
    width = heads * dimension
    halo_spec, own_spec, taps_spec, per_head, slopes = conv_specs(margin, length, dimension, layers)
    return pl.pallas_call(
        functools.partial(conv_back_kernel, margin),
        grid=(3, heads),
        in_specs=[per_head, slopes, taps_spec],
        out_specs=(halo_spec, own_spec),
        out_shape=(
            jax.ShapeDtypeStruct((3, margin, width), jnp.bfloat16),
            jax.ShapeDtypeStruct((3, length, width), jnp.float32),
        ),
        compiler_params=pltpu.CompilerParams(vmem_limit_bytes=32 * 2**20),
        name="conv_backward",
    )(grad, slope, taps)


def unit(rows):
    return rows * lax.rsqrt(jnp.sum(rows * rows, axis=2, keepdims=True) + EPSILON)


def prepare(convolved, log_decay, beta_gate):
    length = log_decay.shape[1]
    queries, keyvec, values = unit(convolved[0]), unit(convolved[1]), convolved[2]
    positions = jnp.arange(length)
    upper_ones = (positions[:, None] <= positions[None, :]).astype(jnp.float32)
    cumulative = jnp.dot(log_decay, upper_ones, precision=EXACT)
    strict_lower_mask = positions[:, None] > positions[None, :]
    log_gaps = jnp.where(
        strict_lower_mask[None], cumulative[:, :, None] - cumulative[:, None, :], 0.0
    )
    affinity = jnp.einsum("htk,hsk->hts", keyvec, keyvec, precision=PRECISE)
    lower_part = jnp.where(strict_lower_mask[None], jnp.exp(log_gaps) * affinity, 0.0)
    dimension = keyvec.shape[2]
    given = jnp.concatenate(
        [beta_gate[:, :, None] * values, (beta_gate * jnp.exp(cumulative))[:, :, None] * keyvec], 2
    )
    found = solved(beta_gate[:, :, None] * lower_part, given)
    pseudo, keyed_rows = found[:, :, :dimension], found[:, :, dimension:]
    group_total = cumulative[:, -1]
    remain = jnp.exp(group_total[:, None] - cumulative)
    transition = jnp.exp(group_total)[:, None, None] * jnp.eye(dimension, dtype=jnp.float32)[
        None
    ] - jnp.einsum("htk,ht,htj->hkj", keyed_rows, remain, keyvec, precision=PRECISE)
    group_state = jnp.einsum("htv,ht,htk->hvk", pseudo, remain, keyvec, precision=PRECISE)
    return (queries, keyvec, cumulative, pseudo, keyed_rows, transition, group_state)


def finish(pieces, entering):
    queries, keyvec, cumulative, pseudo, keyed_rows, transition, group_state = pieces
    length = cumulative.shape[1]
    positions = jnp.arange(length)
    within = positions[:, None] >= positions[None, :]
    log_gaps = jnp.where(within[None], cumulative[:, :, None] - cumulative[:, None, :], 0.0)
    intersection = jnp.einsum("htk,hsk->hts", queries, keyvec, precision=PRECISE)
    weights = jnp.where(within[None], jnp.exp(log_gaps) * intersection, 0.0)
    written = pseudo - jnp.einsum("htk,hvk->htv", keyed_rows, entering, precision=PRECISE)
    scaling = queries.shape[2] ** (-0.5)
    carried_in = jnp.exp(cumulative)[:, :, None] * jnp.einsum(
        "htk,hvk->htv", queries, entering, precision=PRECISE
    )
    outputs = scaling * (
        carried_in + jnp.einsum("hts,hsv->htv", weights, written, precision=PRECISE)
    )
    leaving = jnp.einsum("hvk,hkj->hvj", entering, transition, precision=PRECISE) + group_state
    return (outputs, leaving)


def on_device(token_ids, streams, log_decay, beta_table, conv_weight, cotangent):
    length = streams.shape[1]
    width = streams.shape[2]
    head_count = log_decay.shape[0]
    margin = -(-2 * (2 ** conv_weight.shape[0] - 1) // 16) * 16
    earlier_rows = shifted(streams[:, length - margin :], "seq", 1)
    taps = conv_weight.transpose(2, 0, 1, 3).reshape(3, -1, width)
    first_head = lax.axis_index("grp") * head_count
    own_table = lax.dynamic_slice_in_dim(beta_table, first_head, head_count, 1)
    letters = jnp.arange(beta_table.shape[0])
    one_hot = (letters[:, None] == token_ids[None, :]).astype(jnp.float32)
    beta_gate = jax.nn.sigmoid(jnp.dot(own_table.T, one_hot, precision=EXACT))

    convolved, slope = conv_forward(earlier_rows, streams, taps, head_count)

    def local_pieces(rows_given, decay_given):
        return prepare(rows_given, decay_given, beta_gate)

    pieces, prepare_back = jax.vjp(local_pieces, convolved, log_decay)
    upstream = cotangent.astype(jnp.float32).reshape(length, head_count, -1).transpose(1, 0, 2)
    nothing = jnp.zeros_like(pieces[6])
    state_grad = jax.vjp(lambda state: finish(pieces, state)[0], nothing)[1](upstream)[0]
    entering, later_grad = chain(pieces[5], pieces[6], state_grad)
    (outputs, leaving), finish_back = jax.vjp(finish, pieces, entering)
    summed, unused_grad = finish_back((upstream, later_grad))
    grad_convolved, grad_decay = prepare_back(summed)
    grad_halo, grad_own = conv_backward(grad_convolved, slope, taps, margin)
    returned = shifted(grad_halo, "seq", -1).astype(jnp.float32)
    grad_streams = jnp.concatenate(
        [grad_own[:, : length - margin], grad_own[:, length - margin :] + returned], 1
    )
    mixed_out = outputs.transpose(1, 0, 2).reshape(length, -1).astype(jnp.bfloat16)
    return (mixed_out, grad_streams.astype(jnp.bfloat16), grad_decay)


def solution(mesh):
    placed = (
        P("seq"),
        P(None, "seq", "grp"),
        P("grp", "seq"),
        P(),
        P(None, None, None, "grp"),
        P("seq", "grp"),
    )
    return jax.shard_map(
        on_device,
        mesh=mesh,
        in_specs=placed,
        out_specs=(P("seq", "grp"), P(None, "seq", "grp"), P("grp", "seq")),
        check_vma=False,
    )
```

```python
import jax
import jax.numpy as jnp
from jax import lax
from jax.experimental import pallas as pl
from jax.experimental.pallas import tpu as pltpu
from jax.sharding import PartitionSpec as P
import functools

EXACT = lax.Precision.HIGHEST
PRECISE = lax.Precision.HIGH
TILE = 128
PARTS = 2
EPSILON = 1e-06


def shifted(value, axis, steps):
    count = lax.axis_size(axis)
    first, last = (max(0, -steps), min(count, count - steps))
    return lax.ppermute(value, axis, [(source, source + steps) for source in range(first, last)])


def halves(value):
    high = value.astype(jnp.bfloat16)
    low = (value - high.astype(jnp.float32)).astype(jnp.bfloat16)
    return high, low


def product(left, right, contract=(1, 0)):
    dims = (((contract[0],), (contract[1],)), ((), ()))

    def one(a, b):
        return lax.dot_general(a, b, dims, preferred_element_type=jnp.float32)

    return one(left[0], right[0]) + (one(left[0], right[1]) + one(left[1], right[0]))


def inverse_kernel(lower_ref, inverse_ref):
    length = lower_ref.shape[1]
    count = length // TILE
    rows = lax.broadcasted_iota(jnp.int32, (TILE, TILE), 0)
    columns = lax.broadcasted_iota(jnp.int32, (TILE, TILE), 1)
    identity = (rows == columns).astype(jnp.float32)
    exact = functools.partial(jnp.dot, precision=EXACT, preferred_element_type=jnp.float32)
    cells = [slice(b * TILE, (b + 1) * TILE) for b in range(count)]
    heads = lower_ref.shape[0]
    lowers = [lower_ref[h, cell, cell] for h in range(heads) for cell in cells]
    small = (rows // 8) == (columns // 8)
    firsts = [jnp.where(small, lower, 0.0) for lower in lowers]
    seconds = [exact(first, first) for first in firsts]
    fourths = [exact(second, second) for second in seconds]
    bases = [
        identity - first + second - exact(first, second) for first, second in zip(firsts, seconds)
    ]
    results = [base + exact(base, fourth) for base, fourth in zip(bases, fourths)]
    size = 8
    while size < TILE:
        joined = (rows // (2 * size) == columns // (2 * size)) & (rows // size != columns // size)
        offs = [halves(jnp.where(joined, lower, 0.0)) for lower in lowers]
        splits = [halves(result) for result in results]
        inner = [halves(product(off, split)) for off, split in zip(offs, splits)]
        results = [
            result - product(split, part) for result, split, part in zip(results, splits, inner)
        ]
        size *= 2
    for h in range(heads):
        found = {}
        for i in range(count):
            own = results[h * count + i]
            own_split = halves(own)
            found[i, i] = own_split
            inverse_ref[h, cells[i], cells[i]] = own
            for j in range(i + 1, count):
                inverse_ref[h, cells[i], cells[j]] = jnp.zeros((TILE, TILE), jnp.float32)
            for j in range(i):
                total = jnp.zeros((TILE, TILE), jnp.float32)
                for m in range(j, i):
                    total += product(halves(lower_ref[h, cells[i], cells[m]]), found[m, j])
                entry = -product(own_split, halves(total))
                inverse_ref[h, cells[i], cells[j]] = entry
                found[i, j] = halves(entry)


def inverse_of(lower):
    spec = pl.BlockSpec(memory_space=pltpu.VMEM)
    return pl.pallas_call(
        inverse_kernel,
        in_specs=[spec],
        out_specs=spec,
        out_shape=jax.ShapeDtypeStruct(lower.shape, jnp.float32),
        compiler_params=pltpu.CompilerParams(vmem_limit_bytes=32 * 2**20),
        name="triangle_inverse",
    )(lower)


@jax.custom_vjp
def solved(lower, given):
    return solved_forward(lower, given)[0]


def solved_forward(lower, given):
    inverse = inverse_of(lower)
    found = jnp.einsum("hts,hsk->htk", inverse, given, precision=PRECISE)
    return found, (inverse, found)


def solved_backward(kept, upstream):
    inverse, found = kept
    given_grad = jnp.einsum("hts,htk->hsk", inverse, upstream, precision=PRECISE)
    lower_grad = -jnp.einsum("htk,hsk->hts", given_grad, found, precision=PRECISE)
    return lower_grad, given_grad


solved.defvjp(solved_forward, solved_backward)


def chain_kernel(
    blocks,
    maps,
    states,
    grads,
    entering,
    later,
    high,
    low,
    send_e,
    send_l,
    recv_e,
    recv_l,
    sent_e,
    came_e,
    sent_l,
    came_l,
):
    heads = maps.shape[0]
    me = lax.axis_index("seq")
    right = lax.rem(me + 1, blocks)
    left = lax.rem(me + blocks - 1, blocks)
    has_left = me > 0
    has_right = me < blocks - 1
    barrier = pltpu.get_barrier_semaphore()

    @pl.when(has_left)
    def _():
        pl.semaphore_signal(
            barrier, inc=1, device_id={"seq": left}, device_id_type=pl.DeviceIdType.MESH
        )

    @pl.when(has_right)
    def _():
        pl.semaphore_signal(
            barrier, inc=1, device_id={"seq": right}, device_id_type=pl.DeviceIdType.MESH
        )

    for head in range(heads):
        high[head], low[head] = halves(maps[head])

    @pl.when(has_left & has_right)
    def _():
        pl.semaphore_wait(barrier, 2)

    @pl.when(has_left != has_right)
    def _():
        pl.semaphore_wait(barrier, 1)

    def onward(head):
        return pltpu.make_async_remote_copy(
            src_ref=send_e.at[head],
            dst_ref=recv_e.at[head],
            send_sem=sent_e.at[head],
            recv_sem=came_e.at[head],
            device_id={"seq": right},
            device_id_type=pl.DeviceIdType.MESH,
        )

    def backward(head):
        return pltpu.make_async_remote_copy(
            src_ref=send_l.at[head],
            dst_ref=recv_l.at[head],
            send_sem=sent_l.at[head],
            recv_sem=came_l.at[head],
            device_id={"seq": left},
            device_id_type=pl.DeviceIdType.MESH,
        )

    def pass_on(copy, has_source, has_target, received, sending, kept, added, contract):
        for part in range(heads * PARTS):
            head = part // PARTS

            @pl.when(has_source)
            def _():
                copy(part).wait_recv()
                value = received[part]

                @pl.when(has_target)
                def _():
                    moved = product(halves(value), (high[head], low[head]), contract)
                    sending[part] = moved + added[part]
                    copy(part).start()

                kept[part] = value

            @pl.when(jnp.logical_not(has_source))
            def _():
                @pl.when(has_target)
                def _():
                    sending[part] = added[part]
                    copy(part).start()

                kept[part] = jnp.zeros(kept.shape[1:], jnp.float32)

    def states_on():
        pass_on(onward, has_left, has_right, recv_e, send_e, entering, states, (1, 0))

    def grads_back():
        pass_on(backward, has_right, has_left, recv_l, send_l, later, grads, (1, 1))

    early = me < blocks // 2

    @pl.when(early)
    def _():
        states_on()
        grads_back()

    @pl.when(jnp.logical_not(early))
    def _():
        grads_back()
        states_on()

    for part in range(heads * PARTS):

        @pl.when(has_right)
        def _():
            onward(part).wait_send()

        @pl.when(has_left)
        def _():
            backward(part).wait_send()


def chain(maps, states, grads):
    blocks = lax.axis_size("seq")
    heads, rows, columns = maps.shape
    split = (heads * PARTS, rows // PARTS, columns)
    shape = jax.ShapeDtypeStruct(split, jnp.float32)
    spec = pl.BlockSpec(memory_space=pltpu.VMEM)
    entering, later = pl.pallas_call(
        functools.partial(chain_kernel, blocks),
        out_shape=(shape, shape),
        in_specs=[spec] * 3,
        out_specs=(spec, spec),
        scratch_shapes=[pltpu.VMEM(maps.shape, jnp.bfloat16)] * 2
        + [pltpu.VMEM(split, jnp.float32)] * 4
        + [pltpu.SemaphoreType.DMA((heads * PARTS,))] * 4,
        compiler_params=pltpu.CompilerParams(
            collective_id=0, has_side_effects=True, vmem_limit_bytes=32 * 2**20
        ),
        name="state_chain",
    )(maps, states.reshape(split), grads.reshape(split))
    return entering.reshape(maps.shape), later.reshape(maps.shape)


def conv_kernel(margin, halo_ref, own_ref, taps_ref, out_ref, slope_ref):
    current = jnp.concatenate(
        [halo_ref[0].astype(jnp.float32), own_ref[0].astype(jnp.float32)], 0
    )
    for layer in range(slope_ref.shape[0]):
        spacing = 2**layer
        first, second, third = (taps_ref[0, 3 * layer + i : 3 * layer + i + 1, :] for i in range(3))
        summed = (
            first * current
            + second * pltpu.roll(current, spacing, 0)
            + third * pltpu.roll(current, 2 * spacing, 0)
        )
        gate = 0.5 * jnp.tanh(0.5 * summed) + 0.5
        slope_ref[layer, 0] = gate * (1.0 + summed * (1.0 - gate))
        current = current + summed * gate
    out_ref[0, 0] = current[margin:]


def conv_back_kernel(margin, grad_ref, slope_ref, taps_ref, halo_ref, own_ref):
    grad = grad_ref[0, 0]
    grad = jnp.concatenate([jnp.zeros((margin, grad.shape[1]), jnp.float32), grad], 0)
    extent = grad.shape[0]
    for layer in reversed(range(slope_ref.shape[0])):
        spacing = 2**layer
        first, second, third = (taps_ref[0, 3 * layer + i : 3 * layer + i + 1, :] for i in range(3))
        inner = grad * slope_ref[layer, 0]
        grad = (
            grad
            + first * inner
            + pltpu.roll(second * inner, extent - spacing, 0)
            + pltpu.roll(third * inner, extent - 2 * spacing, 0)
        )
    halo_ref[0] = grad[:margin].astype(jnp.bfloat16)
    own_ref[0] = grad[margin:]


def conv_specs(margin, length, dimension, layers):
    def columns(rows):
        return pl.BlockSpec((1, rows, dimension), lambda s, h: (s, 0, h))

    per_head = pl.BlockSpec((1, 1, length, dimension), lambda s, h: (s, h, 0, 0))
    slopes = pl.BlockSpec((layers, 1, margin + length, dimension), lambda s, h: (0, s, 0, h))
    return columns(margin), columns(length), columns(3 * layers), per_head, slopes


def conv_forward(halo, own, taps, heads):
    margin, length, width = halo.shape[1], own.shape[1], own.shape[2]
    layers, dimension = taps.shape[1] // 3, width // heads
    halo_spec, own_spec, taps_spec, per_head, slopes = conv_specs(margin, length, dimension, layers)
    return pl.pallas_call(
        functools.partial(conv_kernel, margin),
        grid=(3, heads),
        in_specs=[halo_spec, own_spec, taps_spec],
        out_specs=(per_head, slopes),
        out_shape=(
            jax.ShapeDtypeStruct((3, heads, length, dimension), jnp.float32),
            jax.ShapeDtypeStruct((layers, 3, margin + length, width), jnp.float32),
        ),
        compiler_params=pltpu.CompilerParams(vmem_limit_bytes=32 * 2**20),
        name="conv_forward",
    )(halo, own, taps)


def conv_backward(grad, slope, taps, margin):
    heads, length, dimension = grad.shape[1:]
    layers = slope.shape[0]
    width = heads * dimension
    halo_spec, own_spec, taps_spec, per_head, slopes = conv_specs(margin, length, dimension, layers)
    return pl.pallas_call(
        functools.partial(conv_back_kernel, margin),
        grid=(3, heads),
        in_specs=[per_head, slopes, taps_spec],
        out_specs=(halo_spec, own_spec),
        out_shape=(
            jax.ShapeDtypeStruct((3, margin, width), jnp.bfloat16),
            jax.ShapeDtypeStruct((3, length, width), jnp.float32),
        ),
        compiler_params=pltpu.CompilerParams(vmem_limit_bytes=32 * 2**20),
        name="conv_backward",
    )(grad, slope, taps)


def unit(rows):
    return rows * lax.rsqrt(jnp.sum(rows * rows, axis=2, keepdims=True) + EPSILON)


def prepare(convolved, log_decay, beta_gate):
    length = log_decay.shape[1]
    queries, keyvec, values = unit(convolved[0]), unit(convolved[1]), convolved[2]
    positions = jnp.arange(length)
    upper_ones = (positions[:, None] <= positions[None, :]).astype(jnp.float32)
    cumulative = jnp.dot(log_decay, upper_ones, precision=EXACT)
    strict_lower_mask = positions[:, None] > positions[None, :]
    log_gaps = jnp.where(
        strict_lower_mask[None], cumulative[:, :, None] - cumulative[:, None, :], 0.0
    )
    affinity = jnp.einsum("htk,hsk->hts", keyvec, keyvec, precision=PRECISE)
    lower_part = jnp.where(strict_lower_mask[None], jnp.exp(log_gaps) * affinity, 0.0)
    dimension = keyvec.shape[2]
    given = jnp.concatenate(
        [beta_gate[:, :, None] * values, (beta_gate * jnp.exp(cumulative))[:, :, None] * keyvec], 2
    )
    found = solved(beta_gate[:, :, None] * lower_part, given)
    pseudo, keyed_rows = found[:, :, :dimension], found[:, :, dimension:]
    group_total = cumulative[:, -1]
    remain = jnp.exp(group_total[:, None] - cumulative)
    transition = jnp.exp(group_total)[:, None, None] * jnp.eye(dimension, dtype=jnp.float32)[
        None
    ] - jnp.einsum("htk,ht,htj->hkj", keyed_rows, remain, keyvec, precision=PRECISE)
    group_state = jnp.einsum("htv,ht,htk->hvk", pseudo, remain, keyvec, precision=PRECISE)
    return (queries, keyvec, cumulative, pseudo, keyed_rows, transition, group_state)


def finish(pieces, entering):
    queries, keyvec, cumulative, pseudo, keyed_rows, transition, group_state = pieces
    length = cumulative.shape[1]
    positions = jnp.arange(length)
    within = positions[:, None] >= positions[None, :]
    log_gaps = jnp.where(within[None], cumulative[:, :, None] - cumulative[:, None, :], 0.0)
    intersection = jnp.einsum("htk,hsk->hts", queries, keyvec, precision=PRECISE)
    weights = jnp.where(within[None], jnp.exp(log_gaps) * intersection, 0.0)
    written = pseudo - jnp.einsum("htk,hvk->htv", keyed_rows, entering, precision=PRECISE)
    scaling = queries.shape[2] ** (-0.5)
    carried_in = jnp.exp(cumulative)[:, :, None] * jnp.einsum(
        "htk,hvk->htv", queries, entering, precision=PRECISE
    )
    outputs = scaling * (
        carried_in + jnp.einsum("hts,hsv->htv", weights, written, precision=PRECISE)
    )
    leaving = jnp.einsum("hvk,hkj->hvj", entering, transition, precision=PRECISE) + group_state
    return (outputs, leaving)


def on_device(token_ids, streams, log_decay, beta_table, conv_weight, cotangent):
    length = streams.shape[1]
    width = streams.shape[2]
    head_count = log_decay.shape[0]
    margin = -(-2 * (2 ** conv_weight.shape[0] - 1) // 16) * 16
    earlier_rows = shifted(streams[:, length - margin :], "seq", 1)
    taps = conv_weight.transpose(2, 0, 1, 3).reshape(3, -1, width)
    first_head = lax.axis_index("grp") * head_count
    own_table = lax.dynamic_slice_in_dim(beta_table, first_head, head_count, 1)
    letters = jnp.arange(beta_table.shape[0])
    one_hot = (letters[:, None] == token_ids[None, :]).astype(jnp.float32)
    beta_gate = jax.nn.sigmoid(jnp.dot(own_table.T, one_hot, precision=EXACT))

    convolved, slope = conv_forward(earlier_rows, streams, taps, head_count)

    def local_pieces(rows_given, decay_given):
        return prepare(rows_given, decay_given, beta_gate)

    pieces, prepare_back = jax.vjp(local_pieces, convolved, log_decay)
    upstream = cotangent.astype(jnp.float32).reshape(length, head_count, -1).transpose(1, 0, 2)
    nothing = jnp.zeros_like(pieces[6])
    state_grad = jax.vjp(lambda state: finish(pieces, state)[0], nothing)[1](upstream)[0]
    entering, later_grad = chain(pieces[5], pieces[6], state_grad)
    (outputs, leaving), finish_back = jax.vjp(finish, pieces, entering)
    summed, unused_grad = finish_back((upstream, later_grad))
    grad_convolved, grad_decay = prepare_back(summed)
    grad_halo, grad_own = conv_backward(grad_convolved, slope, taps, margin)
    returned = shifted(grad_halo, "seq", -1).astype(jnp.float32)
    grad_streams = jnp.concatenate(
        [grad_own[:, : length - margin], grad_own[:, length - margin :] + returned], 1
    )
    mixed_out = outputs.transpose(1, 0, 2).reshape(length, -1).astype(jnp.bfloat16)
    return (mixed_out, grad_streams.astype(jnp.bfloat16), grad_decay)


def solution(mesh):
    placed = (
        P("seq"),
        P(None, "seq", "grp"),
        P("grp", "seq"),
        P(),
        P(None, None, None, "grp"),
        P("seq", "grp"),
    )
    return jax.shard_map(
        on_device,
        mesh=mesh,
        in_specs=placed,
        out_specs=(P("seq", "grp"), P(None, "seq", "grp"), P("grp", "seq")),
        check_vma=False,
    )
```
